32 devices in a mesh: tm: 8 (over y, x, core), input: 4 (over z).
Axes of the slice: x: 2, y: 2, z: 4, core: 2. Of those that a mesh axis runs over, the one named last changes fastest.
Arguments:
- samples: int32 [1024, 131072], P('input', 'tm'), may hold values from -16 to 16, as said below
- coefficients: float32 [8, 512], replicated, may hold values from -2 to 2
Outputs:
- visibility: bfloat16 [256, 2, 1024, 1024], P(('tm', 'input'))
The draws below stay inside these ranges and needn't reach their ends.
Inputs may be any that keep to these rules, and one draw needn't show every extreme that they name: `samples`: noise-dominated integer voltages: each input carries independent integer noise plus a weak common signal.
All inputs are finite; a program needn't handle non-finite values.
Results may differ from the reference program's by a relative error of at most 0.007.
Values may be sent and summed in bfloat16 or wider, within the bound.
A program may use at most 192 MiB of HBM per device.

```python
import math
import jax
import jax.numpy as jnp
from jax import lax

INPUTS = 1024
NFFT = 512
TAPS = 8
FRAMES = 256
CHANNELS = 256


def draw_samples(key, part):
    keys_all = jax.random.split(key, 4)
    total_len = FRAMES * NFFT
    sky_signal = jax.random.randint(keys_all[0], (total_len + 64,), -2, 3)
    delays = jax.random.randint(keys_all[1], (INPUTS,), 0, 64)
    gains = jax.random.randint(keys_all[2], (INPUTS, 1), 1, 3)
    noise_part = jax.random.randint(keys_all[3], (INPUTS, total_len), -12, 13)

    def shift_row(delay_value):
        return lax.dynamic_slice_in_dim(sky_signal, delay_value, total_len)
    shifted = jax.vmap(shift_row)(delays)
    result_samples = gains * shifted + noise_part
    result_samples = result_samples.at[0, 0].set(16).at[0, 1].set(-16)
    return result_samples.astype(jnp.int32)


def gaussian(own_key, dims, scale, limit, held_as=jnp.bfloat16):
    result = jax.random.normal(own_key, dims, jnp.float32) * scale
    return jnp.minimum(jnp.maximum(result, -limit), limit).astype(held_as)


def setup_inputs(seed: int = 0) -> dict:
    keys = jax.random.split(jax.random.key(seed), 3)
    return {
        "samples": draw_samples(jax.random.fold_in(keys[2], 71), 0),
        "coefficients": gaussian(keys[1], (TAPS, NFFT), TAPS ** -0.5, 2.0, jnp.float32),
    }


def dft_table(length):
    row_index = jnp.arange(length, dtype=jnp.int32)
    channel = row_index // 2
    parity = row_index % 2
    positions = jnp.arange(length, dtype=jnp.int32)
    phase_index = channel[:, None] * positions[None, :] % length
    angles = phase_index.astype(jnp.float32) * (2.0 * math.pi / length)
    values = jnp.where(parity[:, None] == 0, jnp.cos(angles), -jnp.sin(angles)) / math.sqrt(length)
    return values.astype(jnp.bfloat16)

def reference(samples, coefficients):
    signal = samples.astype(jnp.float32) / 8.0
    framed = signal.reshape(INPUTS, FRAMES, NFFT)
    padded = jnp.concatenate([jnp.zeros((INPUTS, TAPS - 1, NFFT), jnp.float32), framed], axis=1)
    filtered = jnp.zeros((INPUTS, FRAMES, NFFT), jnp.float32)
    for tap_index in range(TAPS):
        start_frame = TAPS - 1 - tap_index
        filtered = filtered + coefficients[tap_index][None, None, :] * padded[:, start_frame:start_frame + FRAMES, :]
    filtered = filtered.astype(jnp.bfloat16)
    spectra = jnp.dot(filtered.reshape(INPUTS * FRAMES, NFFT), dft_table(NFFT).T, preferred_element_type=jnp.float32).astype(jnp.bfloat16)
    spectra = spectra.reshape(INPUTS, FRAMES, CHANNELS, 2).transpose(2, 3, 1, 0)

    def correlate_one(channel_block):
        stacked = channel_block.reshape(2 * FRAMES, INPUTS).astype(jnp.float32)
        real_part = jnp.dot(stacked.T, stacked, preferred_element_type=jnp.float32)
        cross_part = jnp.dot(channel_block[1].astype(jnp.float32).T, channel_block[0].astype(jnp.float32), preferred_element_type=jnp.float32)
        imag_part = cross_part - cross_part.T
        return (jnp.stack([real_part, imag_part]) / FRAMES).astype(jnp.bfloat16)
    return lax.map(correlate_one, spectra)
```

```python
import functools
import math

import jax
import jax.numpy as jnp
import ml_dtypes
import numpy as np
from jax import lax
from jax.experimental import pallas as pl
from jax.experimental.pallas import tpu as pltpu
from jax.sharding import PartitionSpec as P

MESH = pl.DeviceIdType.MESH
GROUP = 16
UNIT = 8


def dft_table(length):
    row = np.arange(length)
    phase = ((row // 2)[:, None] * np.arange(length)[None, :]) % length
    angles = phase.astype(np.float32) * np.float32(2.0 * math.pi / length)
    values = np.where((row % 2)[:, None] == 0, np.cos(angles), -np.sin(angles))
    return (values / np.float32(math.sqrt(length))).astype(ml_dtypes.bfloat16)


def reorder_matrix():
    size = GROUP * GROUP
    target = np.arange(size)
    matrix = np.zeros((size, size), np.float32)
    matrix[target, (target % GROUP) * GROUP + target // GROUP] = 1.0
    return matrix.astype(ml_dtypes.bfloat16)


def partner(me, step, count):
    if count & (count - 1):
        return lax.rem(me + step, count)
    result = 0
    bit = 1
    while bit < count:
        flipped = lax.rem(lax.div(me, bit) + lax.div(step, bit), 2)
        result = result + bit * flipped
        bit *= 2
    return result


def exchange_kernel(
    tm_count,
    input_count,
    samples_ref,
    coef_ref,
    table_ref,
    reorder_ref,
    recv_ref,
    stage,
    signal,
    halo_out,
    halo_in,
    filtered,
    spectra,
    send,
    load_sem,
    halo_sem,
    send_sem,
    recv_sem,
    own_sem,
):
    devices = tm_count * input_count
    taps, length = coef_ref.shape
    inputs = samples_ref.shape[0]
    frames = samples_ref.shape[1] // length
    halo = taps - 1
    units = frames // UNIT
    groups = frames // GROUP
    rows = length // devices
    tm = lax.axis_index("tm")
    me = tm * input_count + lax.axis_index("input")

    def load(unit):
        return pltpu.make_async_copy(
            samples_ref.at[:, pl.ds(unit * UNIT * length, UNIT * length)],
            stage.at[unit % 2],
            load_sem.at[unit % 2],
        )

    load(units - 1).start()
    if units > 1:
        load(units - 2).start()

    def place(device):
        return {"tm": lax.div(device, input_count), "input": lax.rem(device, input_count)}

    barrier = pltpu.get_barrier_semaphore()

    def greet(step, carry):
        pl.semaphore_signal(
            barrier, inc=1, device_id=place(partner(me, step, devices)), device_id_type=MESH
        )
        return carry

    lax.fori_loop(1, devices, greet, 0)

    def convert(unit):
        load(unit).wait()
        for frame in range(UNIT):

            def chunk(k, carry):
                at = pl.ds(pl.multiple_of(k * 32, 32), 32)
                values = stage[unit % 2, at, frame * length : (frame + 1) * length]
                values = values.astype(jnp.float32) * 0.125
                signal[halo + unit * UNIT + frame, at, :] = values
                if unit == units - 1 and frame >= UNIT - halo:
                    halo_out[frame - (UNIT - halo), at, :] = values.astype(jnp.bfloat16)
                return carry

            lax.fori_loop(0, inputs // 32, chunk, 0)
        if unit >= 2:
            load(unit - 2).start()

    convert(units - 1)
    pl.semaphore_wait(barrier, devices - 1)
    halo_copy = pltpu.make_async_remote_copy(
        src_ref=halo_out,
        dst_ref=halo_in,
        send_sem=halo_sem.at[0],
        recv_sem=halo_sem.at[1],
        device_id={"tm": lax.rem(tm + 1, tm_count), "input": lax.axis_index("input")},
        device_id_type=MESH,
    )
    halo_copy.start()

    next_unit = units - 2
    for group in reversed(range(groups)):
        first = group * GROUP
        while next_unit >= 0 and (next_unit + 1) * UNIT > first - halo:
            convert(next_unit)
            next_unit -= 1
        if group == 0:
            halo_copy.wait()
            keep = jnp.where(tm == 0, 0.0, 1.0)

            def unpack(index, carry):
                at = pl.ds(pl.multiple_of(lax.rem(index, inputs // 32) * 32, 32), 32)
                frame = lax.div(index, inputs // 32)
                signal[frame, at, :] = halo_in[frame, at, :].astype(jnp.float32) * keep
                return carry

            lax.fori_loop(0, halo * (inputs // 32), unpack, 0)

        def one_frame(frame, carry):
            def chunk(k, inner):
                at = pl.ds(pl.multiple_of(k * 32, 32), 32)
                total = coef_ref[0:1, :] * signal[first + frame + halo, at, :]
                for tap in range(1, taps):
                    total = total + coef_ref[tap : tap + 1, :] * signal[
                        first + frame + halo - tap, at, :
                    ]
                filtered[at, :] = total.astype(jnp.bfloat16)
                return inner

            lax.fori_loop(0, inputs // 32, chunk, 0)
            spectra[frame] = lax.dot_general(
                table_ref[...],
                filtered[...],
                (((1,), (1,)), ((), ())),
                preferred_element_type=jnp.float32,
            ).astype(jnp.bfloat16)
            return carry

        lax.fori_loop(0, GROUP, one_frame, 0)

        def reorder(block):
            at = pl.multiple_of(block * GROUP, GROUP)
            part = spectra[:, pl.ds(at, GROUP), :].reshape(GROUP * GROUP, inputs)
            part = jnp.dot(reorder_ref[...], part, preferred_element_type=jnp.float32)
            part = part.astype(jnp.bfloat16).reshape(GROUP, GROUP, inputs)
            send[group, pl.ds(at, GROUP)] = part

        blocks = rows // GROUP
        if blocks * GROUP != rows:

            def reorder_one(block, carry):
                reorder(block)
                return carry

            lax.fori_loop(0, length // GROUP, reorder_one, 0)

        def send_one(step, carry):
            target = partner(me, step, devices)
            if blocks * GROUP == rows:
                for block in range(blocks):
                    reorder(target * blocks + block)
            pltpu.make_async_remote_copy(
                src_ref=send.at[group, pl.ds(target * rows, rows)],
                dst_ref=recv_ref.at[group, me],
                send_sem=send_sem.at[group],
                recv_sem=recv_sem.at[group],
                device_id=place(target),
                device_id_type=MESH,
            ).start()
            return carry

        lax.fori_loop(1, devices, send_one, 0)
        if blocks * GROUP == rows:
            for block in range(blocks):
                reorder(me * blocks + block)
        pltpu.make_async_copy(
            send.at[group, pl.ds(me * rows, rows)], recv_ref.at[group, me], own_sem.at[group]
        ).start()

    for group in reversed(range(groups)):
        pltpu.make_async_copy(
            send.at[group, pl.ds(me * rows, rows)], recv_ref.at[group, me], own_sem.at[group]
        ).wait()
        sent = send.at[group, pl.ds(0, (devices - 1) * rows)]
        pltpu.make_async_copy(sent, sent, send_sem.at[group]).wait()
        got = recv_ref.at[group, pl.ds(0, devices - 1)]
        pltpu.make_async_copy(got, got, recv_sem.at[group]).wait()


def correlate_kernel(frames_all, recv_ref, out_ref, left, right):
    groups, tm_count, input_count, _, _, _, inputs = recv_ref.shape
    depth = groups * tm_count * GROUP
    width = input_count * inputs
    for z in range(input_count):
        at = slice(z * inputs, (z + 1) * inputs)
        past = slice(width + z * inputs, width + (z + 1) * inputs)
        real = recv_ref[:, :, z, 0, 0].reshape(depth, inputs)
        imag = recv_ref[:, :, z, 0, 1].reshape(depth, inputs)
        right[:depth, at] = real
        right[depth:, at] = imag
        right[:depth, past] = -imag
        right[depth:, past] = real
        left[at, :depth] = real.T
        left[at, depth:] = imag.T
    tile = 256
    columns = 512

    def one_row(k, carry):
        at = pl.ds(pl.multiple_of(k * tile, tile), tile)
        for part in range(2):
            for column in range(0, width, columns):
                start = part * width + column
                total = jnp.dot(
                    left[at, :],
                    right[:, start : start + columns],
                    preferred_element_type=jnp.float32,
                )
                out_ref[0, part, at, column : column + columns] = (
                    total * (1.0 / frames_all)
                ).astype(jnp.bfloat16)
        return carry

    lax.fori_loop(0, width // tile, one_row, 0)


def local(samples, coefficients):
    inputs, sample_count = samples.shape
    taps, length = coefficients.shape
    frames = sample_count // length
    tm_count = lax.axis_size("tm")
    input_count = lax.axis_size("input")
    devices = tm_count * input_count
    groups = frames // GROUP
    rows = length // devices
    per_device = rows // 2
    bf16 = jnp.bfloat16
    vmem = pl.BlockSpec(memory_space=pltpu.VMEM)
    anywhere = pl.BlockSpec(memory_space=pl.ANY)
    received = pl.pallas_call(
        functools.partial(exchange_kernel, tm_count, input_count),
        out_shape=jax.ShapeDtypeStruct((groups, devices, rows, GROUP, inputs), bf16),
        in_specs=[anywhere, vmem, vmem, vmem],
        out_specs=anywhere,
        scratch_shapes=[
            pltpu.VMEM((2, inputs, UNIT * length), jnp.int32),
            pltpu.VMEM((frames + taps - 1, inputs, length), jnp.float32),
            pltpu.VMEM((taps - 1, inputs, length), bf16),
            pltpu.VMEM((taps - 1, inputs, length), bf16),
            pltpu.VMEM((inputs, length), bf16),
            pltpu.VMEM((GROUP, length, inputs), bf16),
            pltpu.VMEM((groups, length, GROUP, inputs), bf16),
            pltpu.SemaphoreType.DMA((2,)),
            pltpu.SemaphoreType.DMA((2,)),
            pltpu.SemaphoreType.DMA((groups,)),
            pltpu.SemaphoreType.DMA((groups,)),
            pltpu.SemaphoreType.DMA((groups,)),
        ],
        compiler_params=pltpu.CompilerParams(
            collective_id=0, has_side_effects=True, vmem_limit_bytes=56 * 2**20
        ),
        name="channelise_exchange",
    )(samples, coefficients, jnp.asarray(dft_table(length)), jnp.asarray(reorder_matrix()))
    received = received.reshape(groups, tm_count, input_count, per_device, 2, GROUP, inputs)
    width = input_count * inputs
    depth = frames * tm_count
    return pl.pallas_call(
        functools.partial(correlate_kernel, depth),
        grid=(per_device,),
        out_shape=jax.ShapeDtypeStruct((per_device, 2, width, width), bf16),
        in_specs=[
            pl.BlockSpec(
                (groups, tm_count, input_count, 1, 2, GROUP, inputs),
                lambda c: (0, 0, 0, c, 0, 0, 0),
            )
        ],
        out_specs=pl.BlockSpec((1, 2, width, width), lambda c: (c, 0, 0, 0)),
        scratch_shapes=[
            pltpu.VMEM((width, 2 * depth), bf16),
            pltpu.VMEM((2 * depth, 2 * width), bf16),
        ],
        compiler_params=pltpu.CompilerParams(vmem_limit_bytes=48 * 2**20),
        name="correlate",
    )(received)


def solution(mesh):
    in_specs = (P("input", "tm"), P())
    out_specs = P(("tm", "input"), None, None, None)
    return jax.shard_map(local, mesh=mesh, in_specs=in_specs, out_specs=out_specs, check_vma=False)
```

```python
import functools
import math

import jax
import jax.numpy as jnp
import ml_dtypes
import numpy as np
from jax import lax
from jax.experimental import pallas as pl
from jax.experimental.pallas import tpu as pltpu
from jax.sharding import PartitionSpec as P

MESH = pl.DeviceIdType.MESH
GROUP = 16
UNIT = 8


def dft_table(length):
    row = np.arange(length)
    phase = ((row // 2)[:, None] * np.arange(length)[None, :]) % length
    angles = phase.astype(np.float32) * np.float32(2.0 * math.pi / length)
    values = np.where((row % 2)[:, None] == 0, np.cos(angles), -np.sin(angles))
    return (values / np.float32(math.sqrt(length))).astype(ml_dtypes.bfloat16)


def reorder_matrix():
    size = GROUP * GROUP
    target = np.arange(size)
    matrix = np.zeros((size, size), np.float32)
    matrix[target, (target % GROUP) * GROUP + target // GROUP] = 1.0
    return matrix.astype(ml_dtypes.bfloat16)


def partner(me, step, count):
    if count & (count - 1):
        return lax.rem(me + step, count)
    result = 0
    bit = 1
    while bit < count:
        flipped = lax.rem(lax.div(me, bit) + lax.div(step, bit), 2)
        result = result + bit * flipped
        bit *= 2
    return result


def exchange_kernel(
    tm_count,
    input_count,
    samples_ref,
    coef_ref,
    table_ref,
    reorder_ref,
    recv_ref,
    stage,
    signal,
    halo_out,
    halo_in,
    filtered_even,
    filtered_odd,
    spectra,
    send,
    load_sem,
    halo_send_sem,
    halo_recv_sem,
    send_sem,
    recv_sem,
    own_sem,
):
    devices = tm_count * input_count
    taps, length = coef_ref.shape
    parts, groups, _, _, lanes = send.shape
    frames = samples_ref.shape[1] // length
    halo = taps - 1
    units = frames // UNIT
    slots = stage.shape[0]
    rows = length // devices
    blocks = rows // GROUP
    tm = lax.axis_index("tm")
    me = tm * input_count + lax.axis_index("input")

    chunks = [(part, group) for group in reversed(range(groups)) for part in range(parts)]
    loads = []
    needs = {}
    for part, group in chunks:
        lowest = max(0, (group * GROUP - halo) // UNIT)
        for unit in reversed(range(lowest, (group + 1) * GROUP // UNIT)):
            if (part, unit) not in loads:
                loads.append((part, unit))
        needs[part, group] = len(loads)

    def load(index):
        part, unit = loads[index]
        return pltpu.make_async_copy(
            samples_ref.at[
                part * lanes : (part + 1) * lanes,
                unit * UNIT * length : (unit + 1) * UNIT * length,
            ],
            stage.at[index % slots],
            load_sem.at[index % slots],
        )

    for index in range(min(slots, len(loads))):
        load(index).start()

    def place(device):
        return {"tm": lax.div(device, input_count), "input": lax.rem(device, input_count)}

    barrier = pltpu.get_barrier_semaphore()

    def greet(step, carry):
        pl.semaphore_signal(
            barrier, inc=1, device_id=place(partner(me, step, devices)), device_id_type=MESH
        )
        return carry

    lax.fori_loop(1, devices, greet, 0)

    def convert(index):
        part, unit = loads[index]
        load(index).wait()
        for frame in range(UNIT):

            def some_rows(k, carry):
                at = pl.ds(pl.multiple_of(k * 32, 32), 32)
                values = stage[index % slots, at, frame * length : (frame + 1) * length]
                values = values.astype(jnp.float32) * 0.125
                signal[part, halo + unit * UNIT + frame, at, :] = values
                if unit == units - 1 and frame >= UNIT - halo:
                    halo_out[part, frame - (UNIT - halo), at, :] = values.astype(jnp.bfloat16)
                return carry

            lax.fori_loop(0, lanes // 32, some_rows, 0)
        if index + slots < len(loads):
            load(index + slots).start()

    def halo_copy(part):
        return pltpu.make_async_remote_copy(
            src_ref=halo_out.at[part],
            dst_ref=halo_in.at[part],
            send_sem=halo_send_sem.at[part],
            recv_sem=halo_recv_sem.at[part],
            device_id={"tm": lax.rem(tm + 1, tm_count), "input": lax.axis_index("input")},
            device_id_type=MESH,
        )

    def own_copy(part, group):
        return pltpu.make_async_copy(
            send.at[part, group, pl.ds(me * rows, rows)],
            recv_ref.at[part, group, me],
            own_sem.at[part, group],
        )

    converted = 0
    greeted = False
    for part, group in chunks:
        first = group * GROUP
        while converted < needs[part, group]:
            convert(converted)
            if loads[converted][1] == units - 1:
                if not greeted:
                    pl.semaphore_wait(barrier, devices - 1)
                    greeted = True
                halo_copy(loads[converted][0]).start()
            converted += 1
        if group == 0:
            halo_copy(part).wait()
            keep = jnp.where(tm == 0, 0.0, 1.0)

            def unpack(index, carry):
                at = pl.ds(pl.multiple_of(lax.rem(index, lanes // 32) * 32, 32), 32)
                frame = lax.div(index, lanes // 32)
                values = halo_in[part, frame, at, :].astype(jnp.float32)
                signal[part, frame, at, :] = values * keep
                return carry

            lax.fori_loop(0, halo * (lanes // 32), unpack, 0)

        def apply_taps(frame, into):
            newest = first + frame + halo
            for row in range(0, lanes, 16):
                total = coef_ref[0:1, :] * signal[part, newest, row : row + 16, :]
                for tap in range(1, taps):
                    total = (
                        total
                        + coef_ref[tap : tap + 1, :]
                        * signal[part, newest - tap, row : row + 16, :]
                    )
                into[row : row + 16, :] = total.astype(jnp.bfloat16)

        def transform(frame, source):
            spectra[frame] = lax.dot_general(
                table_ref[...],
                source[...],
                (((1,), (1,)), ((), ())),
                preferred_element_type=jnp.float32,
            ).astype(jnp.bfloat16)

        apply_taps(0, filtered_even)

        def two_frames(pair, carry):
            transform(2 * pair, filtered_even)
            apply_taps(2 * pair + 1, filtered_odd)
            transform(2 * pair + 1, filtered_odd)
            apply_taps(lax.rem(2 * pair + 2, GROUP), filtered_even)
            return carry

        lax.fori_loop(0, GROUP // 2, two_frames, 0)

        def reorder(block):
            at = pl.multiple_of(block * GROUP, GROUP)
            values = spectra[:, pl.ds(at, GROUP), :].reshape(GROUP * GROUP, lanes)
            values = jnp.dot(reorder_ref[...], values, preferred_element_type=jnp.float32)
            values = values.astype(jnp.bfloat16).reshape(GROUP, GROUP, lanes)
            send[part, group, pl.ds(at, GROUP)] = values

        if blocks * GROUP != rows:

            def reorder_one(block, carry):
                reorder(block)
                return carry

            lax.fori_loop(0, length // GROUP, reorder_one, 0)

        def send_one(step, carry):
            target = partner(me, step, devices)
            if blocks * GROUP == rows:
                for block in range(blocks):
                    reorder(target * blocks + block)
            pltpu.make_async_remote_copy(
                src_ref=send.at[part, group, pl.ds(target * rows, rows)],
                dst_ref=recv_ref.at[part, group, me],
                send_sem=send_sem.at[part, group],
                recv_sem=recv_sem.at[part, group],
                device_id=place(target),
                device_id_type=MESH,
            ).start()
            return carry

        lax.fori_loop(1, devices, send_one, 0)
        if blocks * GROUP == rows:
            for block in range(blocks):
                reorder(me * blocks + block)
        own_copy(part, group).start()

    for part, group in chunks:
        own_copy(part, group).wait()
        sent = send.at[part, group, pl.ds(0, (devices - 1) * rows)]
        pltpu.make_async_copy(sent, sent, send_sem.at[part, group]).wait()
        got = recv_ref.at[part, group, pl.ds(0, devices - 1)]
        pltpu.make_async_copy(got, got, recv_sem.at[part, group]).wait()


def correlate_kernel(frames_all, recv_ref, out_ref):
    parts, groups, tm_count, input_count, _, _, _, lanes = recv_ref.shape
    depth = groups * tm_count * GROUP
    pieces = [(z, part) for z in range(input_count) for part in range(parts)]
    together = max(1, min(len(pieces), 256 // lanes))
    blocks = [pieces[k : k + together] for k in range(0, len(pieces), together)]
    wide = together * lanes

    def gather(block, r):
        found = [recv_ref[part, :, :, z, 0, r].reshape(depth, lanes) for z, part in block]
        return found[0] if len(found) == 1 else jnp.concatenate(found, axis=1)

    for a, block in enumerate(blocks):
        real = gather(block, 0).T
        imag = gather(block, 1).T
        left = jnp.concatenate(
            [jnp.concatenate([real, imag], axis=1), jnp.concatenate([imag, -real], axis=1)], axis=0
        )
        for b, other in enumerate(blocks):
            right = jnp.concatenate([gather(other, 0), gather(other, 1)], axis=0)
            total = jnp.dot(left, right, preferred_element_type=jnp.float32)
            total = (total * (1.0 / frames_all)).astype(jnp.bfloat16)
            rows = slice(a * wide, (a + 1) * wide)
            columns = slice(b * wide, (b + 1) * wide)
            out_ref[0, 0, rows, columns] = total[:wide]
            out_ref[0, 1, rows, columns] = total[wide:]


def local(samples, coefficients):
    inputs, sample_count = samples.shape
    taps, length = coefficients.shape
    frames = sample_count // length
    tm_count = lax.axis_size("tm")
    input_count = lax.axis_size("input")
    devices = tm_count * input_count
    groups = frames // GROUP
    lanes = 128
    parts = inputs // lanes
    rows = length // devices
    per_device = rows // 2
    bf16 = jnp.bfloat16
    vmem = pl.BlockSpec(memory_space=pltpu.VMEM)
    anywhere = pl.BlockSpec(memory_space=pl.ANY)
    slots = 4
    received = pl.pallas_call(
        functools.partial(exchange_kernel, tm_count, input_count),
        out_shape=jax.ShapeDtypeStruct((parts, groups, devices, rows, GROUP, lanes), bf16),
        in_specs=[anywhere, vmem, vmem, vmem],
        out_specs=anywhere,
        scratch_shapes=[
            pltpu.VMEM((slots, lanes, UNIT * length), jnp.int32),
            pltpu.VMEM((parts, frames + taps - 1, lanes, length), jnp.float32),
            pltpu.VMEM((parts, taps - 1, lanes, length), bf16),
            pltpu.VMEM((parts, taps - 1, lanes, length), bf16),
            pltpu.VMEM((lanes, length), bf16),
            pltpu.VMEM((lanes, length), bf16),
            pltpu.VMEM((GROUP, length, lanes), bf16),
            pltpu.VMEM((parts, groups, length, GROUP, lanes), bf16),
            pltpu.SemaphoreType.DMA((slots,)),
            pltpu.SemaphoreType.DMA((parts,)),
            pltpu.SemaphoreType.DMA((parts,)),
            pltpu.SemaphoreType.DMA((parts, groups)),
            pltpu.SemaphoreType.DMA((parts, groups)),
            pltpu.SemaphoreType.DMA((parts, groups)),
        ],
        compiler_params=pltpu.CompilerParams(
            collective_id=0, has_side_effects=True, vmem_limit_bytes=56 * 2**20
        ),
        name="channelise_exchange",
    )(samples, coefficients, jnp.asarray(dft_table(length)), jnp.asarray(reorder_matrix()))
    received = received.reshape(
        parts, groups, tm_count, input_count, per_device, 2, GROUP, lanes
    )
    width = input_count * inputs
    return pl.pallas_call(
        functools.partial(correlate_kernel, frames * tm_count),
        grid=(per_device,),
        out_shape=jax.ShapeDtypeStruct((per_device, 2, width, width), bf16),
        in_specs=[
            pl.BlockSpec(
                (parts, groups, tm_count, input_count, 1, 2, GROUP, lanes),
                lambda c: (0, 0, 0, 0, c, 0, 0, 0),
            )
        ],
        out_specs=pl.BlockSpec((1, 2, width, width), lambda c: (c, 0, 0, 0)),
        compiler_params=pltpu.CompilerParams(vmem_limit_bytes=48 * 2**20),
        name="correlate",
    )(received)


def solution(mesh):
    in_specs = (P("input", "tm"), P())
    out_specs = P(("tm", "input"), None, None, None)
    return jax.shard_map(local, mesh=mesh, in_specs=in_specs, out_specs=out_specs, check_vma=False)
```

```python
import functools
import math

import jax
import jax.numpy as jnp
import ml_dtypes
import numpy as np
from jax import lax
from jax.experimental import pallas as pl
from jax.experimental.pallas import tpu as pltpu
from jax.sharding import PartitionSpec as P

MESH = pl.DeviceIdType.MESH
GROUP = 16
UNIT = 8


def dft_table(length):
    row = np.arange(length)
    phase = ((row // 2)[:, None] * np.arange(length)[None, :]) % length
    angles = phase.astype(np.float32) * np.float32(2.0 * math.pi / length)
    values = np.where((row % 2)[:, None] == 0, np.cos(angles), -np.sin(angles))
    return (values / np.float32(math.sqrt(length))).astype(ml_dtypes.bfloat16)


def reorder_matrix():
    size = GROUP * GROUP
    target = np.arange(size)
    matrix = np.zeros((size, size), np.float32)
    matrix[target, (target % GROUP) * GROUP + target // GROUP] = 1.0
    return matrix.astype(ml_dtypes.bfloat16)


def partner(me, step, count):
    if count & (count - 1):
        return lax.rem(me + step, count)
    result = 0
    bit = 1
    while bit < count:
        flipped = lax.rem(lax.div(me, bit) + lax.div(step, bit), 2)
        result = result + bit * flipped
        bit *= 2
    return result


def exchange_kernel(
    tm_count,
    input_count,
    samples_ref,
    coef_ref,
    table_ref,
    reorder_ref,
    recv_ref,
    stage,
    signal,
    halo_out,
    halo_in,
    filtered_even,
    filtered_odd,
    spectra,
    send,
    load_sem,
    halo_send_sem,
    halo_recv_sem,
    send_sem,
    recv_sem,
    own_sem,
):
    devices = tm_count * input_count
    taps, length = coef_ref.shape
    parts, groups, _, _, lanes = send.shape
    frames = samples_ref.shape[1] // length
    halo = taps - 1
    units = frames // UNIT
    slots = stage.shape[0]
    rows = length // devices
    blocks = rows // GROUP
    tm = lax.axis_index("tm")
    me = tm * input_count + lax.axis_index("input")

    chunks = [(part, group) for group in reversed(range(groups)) for part in range(parts)]
    loads = []
    needs = {}
    for part, group in chunks:
        lowest = max(0, (group * GROUP - halo) // UNIT)
        for unit in reversed(range(lowest, (group + 1) * GROUP // UNIT)):
            if (part, unit) not in loads:
                loads.append((part, unit))
        needs[part, group] = len(loads)

    def load(index):
        part, unit = loads[index]
        return pltpu.make_async_copy(
            samples_ref.at[
                part * lanes : (part + 1) * lanes,
                unit * UNIT * length : (unit + 1) * UNIT * length,
            ],
            stage.at[index % slots],
            load_sem.at[index % slots],
        )

    for index in range(min(slots, len(loads))):
        load(index).start()

    def place(device):
        return {"tm": lax.div(device, input_count), "input": lax.rem(device, input_count)}

    barrier = pltpu.get_barrier_semaphore()

    def greet(step, carry):
        pl.semaphore_signal(
            barrier, inc=1, device_id=place(partner(me, step, devices)), device_id_type=MESH
        )
        return carry

    lax.fori_loop(1, devices, greet, 0)

    def convert(index):
        part, unit = loads[index]
        load(index).wait()
        for frame in range(UNIT):

            def some_rows(k, carry):
                at = pl.ds(pl.multiple_of(k * 32, 32), 32)
                values = stage[index % slots, at, frame * length : (frame + 1) * length]
                values = values.astype(jnp.float32) * 0.125
                signal[part, halo + unit * UNIT + frame, at, :] = values
                if unit == units - 1 and frame >= UNIT - halo:
                    halo_out[part, frame - (UNIT - halo), at, :] = values.astype(jnp.bfloat16)
                return carry

            lax.fori_loop(0, lanes // 32, some_rows, 0)
        if index + slots < len(loads):
            load(index + slots).start()

    def halo_copy(part):
        return pltpu.make_async_remote_copy(
            src_ref=halo_out.at[part],
            dst_ref=halo_in.at[part],
            send_sem=halo_send_sem.at[part],
            recv_sem=halo_recv_sem.at[part],
            device_id={"tm": lax.rem(tm + 1, tm_count), "input": lax.axis_index("input")},
            device_id_type=MESH,
        )

    def own_copy(part, group):
        return pltpu.make_async_copy(
            send.at[part, group, pl.ds(me * rows, rows)],
            recv_ref.at[part, group, me],
            own_sem.at[part, group],
        )

    converted = 0
    greeted = False
    for part, group in chunks:
        first = group * GROUP
        while converted < needs[part, group]:
            convert(converted)
            if loads[converted][1] == units - 1:
                if not greeted:
                    pl.semaphore_wait(barrier, devices - 1)
                    greeted = True
                halo_copy(loads[converted][0]).start()
            converted += 1
        if group == 0:
            halo_copy(part).wait()
            keep = jnp.where(tm == 0, 0.0, 1.0)

            def unpack(index, carry):
                at = pl.ds(pl.multiple_of(lax.rem(index, lanes // 32) * 32, 32), 32)
                frame = lax.div(index, lanes // 32)
                values = halo_in[part, frame, at, :].astype(jnp.float32)
                signal[part, frame, at, :] = values * keep
                return carry

            lax.fori_loop(0, halo * (lanes // 32), unpack, 0)

        def apply_taps(frame, into):
            newest = first + frame + halo
            for row in range(0, lanes, 16):
                total = coef_ref[0:1, :] * signal[part, newest, row : row + 16, :]
                for tap in range(1, taps):
                    total = (
                        total
                        + coef_ref[tap : tap + 1, :]
                        * signal[part, newest - tap, row : row + 16, :]
                    )
                into[row : row + 16, :] = total.astype(jnp.bfloat16)

        def transform(frame, source):
            spectra[frame] = lax.dot_general(
                table_ref[...],
                source[...],
                (((1,), (1,)), ((), ())),
                preferred_element_type=jnp.float32,
            ).astype(jnp.bfloat16)

        apply_taps(0, filtered_even)

        def two_frames(pair, carry):
            transform(2 * pair, filtered_even)
            apply_taps(2 * pair + 1, filtered_odd)
            transform(2 * pair + 1, filtered_odd)
            apply_taps(lax.rem(2 * pair + 2, GROUP), filtered_even)
            return carry

        lax.fori_loop(0, GROUP // 2, two_frames, 0)

        def reorder(block):
            at = pl.multiple_of(block * GROUP, GROUP)
            values = spectra[:, pl.ds(at, GROUP), :].reshape(GROUP * GROUP, lanes)
            values = jnp.dot(reorder_ref[...], values, preferred_element_type=jnp.float32)
            values = values.astype(jnp.bfloat16).reshape(GROUP, GROUP, lanes)
            send[part, group, pl.ds(at, GROUP)] = values

        if blocks * GROUP != rows:

            def reorder_one(block, carry):
                reorder(block)
                return carry

            lax.fori_loop(0, length // GROUP, reorder_one, 0)

        def send_one(step, carry):
            target = partner(me, step, devices)
            if blocks * GROUP == rows:
                for block in range(blocks):
                    reorder(target * blocks + block)
            pltpu.make_async_remote_copy(
                src_ref=send.at[part, group, pl.ds(target * rows, rows)],
                dst_ref=recv_ref.at[part, group, me],
                send_sem=send_sem.at[part, group],
                recv_sem=recv_sem.at[part, group],
                device_id=place(target),
                device_id_type=MESH,
            ).start()
            return carry

        half = input_count // 2
        if half and not (devices & (devices - 1)):

            def send_varied(step, carry):
                across = lax.rem(lax.div(step, half), 2)
                return send_one(step + lax.rem(tm, 2) * half * (1 - 2 * across), carry)

            send_one(half, 0)
            lax.fori_loop(1, half, send_varied, 0)
            lax.fori_loop(half + 1, devices, send_varied, 0)
        else:
            lax.fori_loop(1, devices, send_one, 0)
        if blocks * GROUP == rows:
            for block in range(blocks):
                reorder(me * blocks + block)
        own_copy(part, group).start()

    for part, group in chunks:
        own_copy(part, group).wait()
        sent = send.at[part, group, pl.ds(0, (devices - 1) * rows)]
        pltpu.make_async_copy(sent, sent, send_sem.at[part, group]).wait()
        got = recv_ref.at[part, group, pl.ds(0, devices - 1)]
        pltpu.make_async_copy(got, got, recv_sem.at[part, group]).wait()


def correlate_kernel(frames_all, recv_ref, out_ref):
    parts, groups, tm_count, input_count, _, _, _, lanes = recv_ref.shape
    depth = groups * tm_count * GROUP
    pieces = [(z, part) for z in range(input_count) for part in range(parts)]
    together = max(1, min(len(pieces), 256 // lanes))
    blocks = [pieces[k : k + together] for k in range(0, len(pieces), together)]
    wide = together * lanes

    def gather(block, r):
        found = [recv_ref[part, :, :, z, 0, r].reshape(depth, lanes) for z, part in block]
        return found[0] if len(found) == 1 else jnp.concatenate(found, axis=1)

    def slices(a, b):
        return slice(a * wide, (a + 1) * wide), slice(b * wide, (b + 1) * wide)

    def mirror(a, b):
        rows, columns = slices(a, b)
        out_ref[0, 0, columns, rows] = out_ref[0, 0, rows, columns].T
        out_ref[0, 1, columns, rows] = -out_ref[0, 1, rows, columns].T

    waiting = None
    for a, block in enumerate(blocks):
        real = gather(block, 0).T
        imag = gather(block, 1).T
        left = jnp.concatenate(
            [jnp.concatenate([real, imag], axis=1), jnp.concatenate([imag, -real], axis=1)], axis=0
        )
        for b in range(a, len(blocks)):
            right = jnp.concatenate([gather(blocks[b], 0), gather(blocks[b], 1)], axis=0)
            total = jnp.dot(left, right, preferred_element_type=jnp.float32)
            total = (total * (1.0 / frames_all)).astype(jnp.bfloat16)
            rows, columns = slices(a, b)
            out_ref[0, 0, rows, columns] = total[:wide]
            out_ref[0, 1, rows, columns] = total[wide:]
            if waiting:
                mirror(*waiting)
            waiting = (a, b) if b > a else None
    if waiting:
        mirror(*waiting)


def local(samples, coefficients):
    inputs, sample_count = samples.shape
    taps, length = coefficients.shape
    frames = sample_count // length
    tm_count = lax.axis_size("tm")
    input_count = lax.axis_size("input")
    devices = tm_count * input_count
    groups = frames // GROUP
    lanes = 128
    parts = inputs // lanes
    rows = length // devices
    per_device = rows // 2
    bf16 = jnp.bfloat16
    vmem = pl.BlockSpec(memory_space=pltpu.VMEM)
    anywhere = pl.BlockSpec(memory_space=pl.ANY)
    slots = 4
    received = pl.pallas_call(
        functools.partial(exchange_kernel, tm_count, input_count),
        out_shape=jax.ShapeDtypeStruct((parts, groups, devices, rows, GROUP, lanes), bf16),
        in_specs=[anywhere, vmem, vmem, vmem],
        out_specs=anywhere,
        scratch_shapes=[
            pltpu.VMEM((slots, lanes, UNIT * length), jnp.int32),
            pltpu.VMEM((parts, frames + taps - 1, lanes, length), jnp.float32),
            pltpu.VMEM((parts, taps - 1, lanes, length), bf16),
            pltpu.VMEM((parts, taps - 1, lanes, length), bf16),
            pltpu.VMEM((lanes, length), bf16),
            pltpu.VMEM((lanes, length), bf16),
            pltpu.VMEM((GROUP, length, lanes), bf16),
            pltpu.VMEM((parts, groups, length, GROUP, lanes), bf16),
            pltpu.SemaphoreType.DMA((slots,)),
            pltpu.SemaphoreType.DMA((parts,)),
            pltpu.SemaphoreType.DMA((parts,)),
            pltpu.SemaphoreType.DMA((parts, groups)),
            pltpu.SemaphoreType.DMA((parts, groups)),
            pltpu.SemaphoreType.DMA((parts, groups)),
        ],
        compiler_params=pltpu.CompilerParams(
            collective_id=0, has_side_effects=True, vmem_limit_bytes=56 * 2**20
        ),
        name="channelise_exchange",
    )(samples, coefficients, jnp.asarray(dft_table(length)), jnp.asarray(reorder_matrix()))
    received = received.reshape(
        parts, groups, tm_count, input_count, per_device, 2, GROUP, lanes
    )
    width = input_count * inputs
    return pl.pallas_call(
        functools.partial(correlate_kernel, frames * tm_count),
        grid=(per_device,),
        out_shape=jax.ShapeDtypeStruct((per_device, 2, width, width), bf16),
        in_specs=[
            pl.BlockSpec(
                (parts, groups, tm_count, input_count, 1, 2, GROUP, lanes),
                lambda c: (0, 0, 0, 0, c, 0, 0, 0),
            )
        ],
        out_specs=pl.BlockSpec((1, 2, width, width), lambda c: (c, 0, 0, 0)),
        compiler_params=pltpu.CompilerParams(vmem_limit_bytes=48 * 2**20),
        name="correlate",
    )(received)


def solution(mesh):
    in_specs = (P("input", "tm"), P())
    out_specs = P(("tm", "input"), None, None, None)
    return jax.shard_map(local, mesh=mesh, in_specs=in_specs, out_specs=out_specs, check_vma=False)
```

```python
import functools
import math

import jax
import jax.numpy as jnp
import ml_dtypes
import numpy as np
from jax import lax
from jax.experimental import pallas as pl
from jax.experimental.pallas import tpu as pltpu
from jax.sharding import PartitionSpec as P

MESH = pl.DeviceIdType.MESH
GROUP = 16
UNIT = 8


def dft_table(length):
    row = np.arange(length)
    phase = ((row // 2)[:, None] * np.arange(length)[None, :]) % length
    angles = phase.astype(np.float32) * np.float32(2.0 * math.pi / length)
    values = np.where((row % 2)[:, None] == 0, np.cos(angles), -np.sin(angles))
    return (values / np.float32(math.sqrt(length))).astype(ml_dtypes.bfloat16)


def reorder_matrix():
    size = GROUP * GROUP
    target = np.arange(size)
    matrix = np.zeros((size, size), np.float32)
    matrix[target, (target % GROUP) * GROUP + target // GROUP] = 1.0
    return matrix.astype(ml_dtypes.bfloat16)


def partner(me, step, count):
    if count & (count - 1):
        return lax.rem(me + step, count)
    result = 0
    bit = 1
    while bit < count:
        flipped = lax.rem(lax.div(me, bit) + lax.div(step, bit), 2)
        result = result + bit * flipped
        bit *= 2
    return result


def exchange_kernel(
    tm_count,
    input_count,
    samples_ref,
    coef_ref,
    table_ref,
    reorder_ref,
    recv_ref,
    early_ref,
    stage,
    signal,
    halo_out,
    halo_in,
    filtered_even,
    filtered_odd,
    spectra,
    send,
    load_sem,
    halo_send_sem,
    halo_recv_sem,
    send_sem,
    recv_sem,
    own_sem,
    late_sem,
    block,
    block_sem,
):
    early = early_ref.shape[0]
    early_rows = 2 * early
    devices = tm_count * input_count
    taps, length = coef_ref.shape
    parts, groups, _, _, lanes = send.shape
    frames = samples_ref.shape[1] // length
    halo = taps - 1
    units = frames // UNIT
    slots = stage.shape[0]
    rows = length // devices
    blocks = rows // GROUP
    tm = lax.axis_index("tm")
    me = tm * input_count + lax.axis_index("input")

    chunks = [(part, group) for part in range(parts) for group in reversed(range(groups))]
    loads = []
    needs = {}
    for part, group in chunks:
        lowest = max(0, (group * GROUP - halo) // UNIT)
        for unit in reversed(range(lowest, (group + 1) * GROUP // UNIT)):
            if (part, unit) not in loads:
                loads.append((part, unit))
        needs[part, group] = len(loads)

    def load(index):
        part, unit = loads[index]
        return pltpu.make_async_copy(
            samples_ref.at[
                part * lanes : (part + 1) * lanes,
                unit * UNIT * length : (unit + 1) * UNIT * length,
            ],
            stage.at[index % slots],
            load_sem.at[index % slots],
        )

    for index in range(min(slots, len(loads))):
        load(index).start()

    def place(device):
        return {"tm": lax.div(device, input_count), "input": lax.rem(device, input_count)}

    barrier = pltpu.get_barrier_semaphore()

    def greet(step, carry):
        pl.semaphore_signal(
            barrier, inc=1, device_id=place(partner(me, step, devices)), device_id_type=MESH
        )
        return carry

    lax.fori_loop(1, devices, greet, 0)

    def convert(index):
        part, unit = loads[index]
        load(index).wait()
        for frame in range(UNIT):

            def some_rows(k, carry):
                at = pl.ds(pl.multiple_of(k * 32, 32), 32)
                values = stage[index % slots, at, frame * length : (frame + 1) * length]
                values = values.astype(jnp.float32) * 0.125
                signal[halo + unit * UNIT + frame, at, :] = values
                if unit == units - 1 and frame >= UNIT - halo:
                    halo_out[part, frame - (UNIT - halo), at, :] = values.astype(jnp.bfloat16)
                return carry

            lax.fori_loop(0, lanes // 32, some_rows, 0)
        if index + slots < len(loads):
            load(index + slots).start()

    def halo_copy(part):
        return pltpu.make_async_remote_copy(
            src_ref=halo_out.at[part],
            dst_ref=halo_in.at[part],
            send_sem=halo_send_sem.at[part],
            recv_sem=halo_recv_sem.at[part],
            device_id={"tm": lax.rem(tm + 1, tm_count), "input": lax.axis_index("input")},
            device_id_type=MESH,
        )

    def own_copy(part, group):
        return pltpu.make_async_copy(
            send.at[part, group, pl.ds(me * rows, rows)],
            recv_ref.at[part, group, me],
            own_sem.at[part, group],
        )

    def to_all(send_one):
        half = input_count // 2
        if half and not (devices & (devices - 1)):

            def send_varied(step, carry):
                across = lax.rem(lax.div(step, half), 2)
                return send_one(step + lax.rem(tm, 2) * half * (1 - 2 * across), carry)

            send_one(half, 0)
            lax.fori_loop(1, half, send_varied, 0)
            lax.fori_loop(half + 1, devices, send_varied, 0)
        else:
            lax.fori_loop(1, devices, send_one, 0)

    converted = 0
    greeted = False
    for part, group in chunks:
        first = group * GROUP
        while converted < needs[part, group]:
            convert(converted)
            if loads[converted][1] == units - 1:
                if not greeted:
                    pl.semaphore_wait(barrier, devices - 1)
                    greeted = True
                halo_copy(loads[converted][0]).start()
            converted += 1
        if group == 0:
            halo_copy(part).wait()
            keep = jnp.where(tm == 0, 0.0, 1.0)

            def unpack(index, carry):
                at = pl.ds(pl.multiple_of(lax.rem(index, lanes // 32) * 32, 32), 32)
                frame = lax.div(index, lanes // 32)
                values = halo_in[part, frame, at, :].astype(jnp.float32)
                signal[frame, at, :] = values * keep
                return carry

            lax.fori_loop(0, halo * (lanes // 32), unpack, 0)

        def apply_taps(frame, into):
            newest = first + frame + halo
            for row in range(0, lanes, 16):
                total = coef_ref[0:1, :] * signal[newest, row : row + 16, :]
                for tap in range(1, taps):
                    total = (
                        total
                        + coef_ref[tap : tap + 1, :]
                        * signal[newest - tap, row : row + 16, :]
                    )
                into[row : row + 16, :] = total.astype(jnp.bfloat16)

        def transform(frame, source):
            spectra[frame] = lax.dot_general(
                table_ref[...],
                source[...],
                (((1,), (1,)), ((), ())),
                preferred_element_type=jnp.float32,
            ).astype(jnp.bfloat16)

        apply_taps(0, filtered_even)

        def two_frames(pair, carry):
            transform(2 * pair, filtered_even)
            apply_taps(2 * pair + 1, filtered_odd)
            transform(2 * pair + 1, filtered_odd)
            apply_taps(lax.rem(2 * pair + 2, GROUP), filtered_even)
            return carry

        lax.fori_loop(0, GROUP // 2, two_frames, 0)

        def reorder(index):
            at = pl.multiple_of(index * GROUP, GROUP)
            values = spectra[:, pl.ds(at, GROUP), :].reshape(GROUP * GROUP, lanes)
            values = jnp.dot(reorder_ref[...], values, preferred_element_type=jnp.float32)
            values = values.astype(jnp.bfloat16).reshape(GROUP, GROUP, lanes)
            send[part, group, pl.ds(at, GROUP)] = values

        if blocks * GROUP != rows:

            def reorder_one(index, carry):
                reorder(index)
                return carry

            lax.fori_loop(0, length // GROUP, reorder_one, 0)

        def send_one(step, carry):
            target = partner(me, step, devices)
            if blocks * GROUP == rows:
                for own in range(blocks):
                    reorder(target * blocks + own)
            pltpu.make_async_remote_copy(
                src_ref=send.at[part, group, pl.ds(target * rows, early_rows)],
                dst_ref=recv_ref.at[part, group, me, pl.ds(0, early_rows)],
                send_sem=send_sem.at[part, group],
                recv_sem=recv_sem.at[part, group],
                device_id=place(target),
                device_id_type=MESH,
            ).start()
            return carry

        to_all(send_one)
        if blocks * GROUP == rows:
            for own in range(blocks):
                reorder(me * blocks + own)
        own_copy(part, group).start()

    def send_late(step, carry):
        target = partner(me, step, devices)
        pltpu.make_async_remote_copy(
            src_ref=send.at[:, :, pl.ds(target * rows + early_rows, rows - early_rows)],
            dst_ref=recv_ref.at[:, :, me, pl.ds(early_rows, rows - early_rows)],
            send_sem=late_sem.at[0],
            recv_sem=late_sem.at[1],
            device_id=place(target),
            device_id_type=MESH,
        ).start()
        return carry

    to_all(send_late)

    for part, group in chunks:
        own_copy(part, group).wait()
        got = recv_ref.at[part, group, pl.ds(0, devices - 1), pl.ds(0, early_rows)]
        pltpu.make_async_copy(got, got, recv_sem.at[part, group]).wait()

    def fetch(channel, slot):
        return pltpu.make_async_copy(
            recv_ref.at[:, :, :, pl.ds(2 * channel, 2)], block.at[slot], block_sem.at[slot]
        )

    fetch(0, 0).start()

    def correlate_one(channel, carry):
        slot = lax.rem(channel, 2)
        fetch(channel, slot).wait()

        @pl.when(channel + 1 < early)
        def _():
            fetch(channel + 1, 1 - slot).start()

        correlate(tm_count, input_count, block.at[slot], early_ref.at[channel])
        return carry

    lax.fori_loop(0, early, correlate_one, 0)

    for part, group in chunks:
        sent = send.at[part, group, pl.ds(0, (devices - 1) * early_rows)]
        pltpu.make_async_copy(sent, sent, send_sem.at[part, group]).wait()
    sent = send.at[:, :, pl.ds(0, (devices - 1) * (rows - early_rows))]
    pltpu.make_async_copy(sent, sent, late_sem.at[0]).wait()
    got = recv_ref.at[:, :, pl.ds(0, devices - 1), pl.ds(early_rows, rows - early_rows)]
    pltpu.make_async_copy(got, got, late_sem.at[1]).wait()


def correlate(tm_count, input_count, block_ref, out_ref):
    parts, groups, _, _, _, lanes = block_ref.shape
    frames_all = groups * tm_count * GROUP
    pieces = [(z, part) for z in range(input_count) for part in range(parts)]
    together = max(1, min(len(pieces), 256 // lanes))
    blocks = [pieces[k : k + together] for k in range(0, len(pieces), together)]
    wide = together * lanes

    def gather(block, r):
        found = [
            jnp.concatenate(
                [
                    block_ref[part, group, t * input_count + z, r]
                    for group in range(groups)
                    for t in range(tm_count)
                ],
                axis=0,
            )
            for z, part in block
        ]
        return found[0] if len(found) == 1 else jnp.concatenate(found, axis=1)

    def slices(a, b):
        return slice(a * wide, (a + 1) * wide), slice(b * wide, (b + 1) * wide)

    def mirror(a, b):
        rows, columns = slices(a, b)
        out_ref[0, columns, rows] = out_ref[0, rows, columns].T
        out_ref[1, columns, rows] = -out_ref[1, rows, columns].T

    waiting = None
    for a, one in enumerate(blocks):
        real = gather(one, 0).T
        imag = gather(one, 1).T
        left = jnp.concatenate(
            [jnp.concatenate([real, imag], axis=1), jnp.concatenate([imag, -real], axis=1)], axis=0
        )
        for b in range(a, len(blocks)):
            right = jnp.concatenate([gather(blocks[b], 0), gather(blocks[b], 1)], axis=0)
            total = jnp.dot(left, right, preferred_element_type=jnp.float32)
            total = (total * (1.0 / frames_all)).astype(jnp.bfloat16)
            rows, columns = slices(a, b)
            out_ref[0, rows, columns] = total[:wide]
            out_ref[1, rows, columns] = total[wide:]
            if waiting:
                mirror(*waiting)
            waiting = (a, b) if b > a else None
    if waiting:
        mirror(*waiting)


def finish_kernel(
    tm_count, input_count, recv_ref, early_ref, out_ref, block, late, block_sem, out_sem
):
    early = early_ref.shape[0]
    count = out_ref.shape[0] - early

    def fetch(k):
        return pltpu.make_async_copy(
            recv_ref.at[:, :, :, 2 * (early + k) : 2 * (early + k) + 2], block.at[k], block_sem.at[k]
        )

    def write(channel):
        source = early_ref.at[channel] if channel < early else late.at[channel - early]
        return pltpu.make_async_copy(source, out_ref.at[channel], out_sem.at[channel])

    for k in range(count):
        fetch(k).start()
    for channel in range(early):
        write(channel).start()
    for k in range(count):
        fetch(k).wait()
        correlate(tm_count, input_count, block.at[k], late.at[k])
        write(early + k).start()
    for channel in range(early + count):
        write(channel).wait()


def local(samples, coefficients):
    inputs, sample_count = samples.shape
    taps, length = coefficients.shape
    frames = sample_count // length
    tm_count = lax.axis_size("tm")
    input_count = lax.axis_size("input")
    devices = tm_count * input_count
    groups = frames // GROUP
    lanes = 128
    parts = inputs // lanes
    rows = length // devices
    per_device = rows // 2
    bf16 = jnp.bfloat16
    vmem = pl.BlockSpec(memory_space=pltpu.VMEM)
    anywhere = pl.BlockSpec(memory_space=pl.ANY)
    hbm = pl.BlockSpec(memory_space=pltpu.HBM)
    slots = 2
    width = input_count * inputs
    early = max(1, per_device * 3 // 4)
    block = (parts, groups, devices, 2, GROUP, lanes)
    received, products = pl.pallas_call(
        functools.partial(exchange_kernel, tm_count, input_count),
        out_shape=(
            jax.ShapeDtypeStruct((parts, groups, devices, rows, GROUP, lanes), bf16),
            pltpu.VMEM((early, 2, width, width), bf16),
        ),
        in_specs=[hbm, vmem, vmem, vmem],
        out_specs=(hbm, vmem),
        scratch_shapes=[
            pltpu.VMEM((slots, lanes, UNIT * length), jnp.int32),
            pltpu.VMEM((frames + taps - 1, lanes, length), jnp.float32),
            pltpu.VMEM((parts, taps - 1, lanes, length), bf16),
            pltpu.VMEM((parts, taps - 1, lanes, length), bf16),
            pltpu.VMEM((lanes, length), bf16),
            pltpu.VMEM((lanes, length), bf16),
            pltpu.VMEM((GROUP, length, lanes), bf16),
            pltpu.VMEM((parts, groups, length, GROUP, lanes), bf16),
            pltpu.SemaphoreType.DMA((slots,)),
            pltpu.SemaphoreType.DMA((parts,)),
            pltpu.SemaphoreType.DMA((parts,)),
            pltpu.SemaphoreType.DMA((parts, groups)),
            pltpu.SemaphoreType.DMA((parts, groups)),
            pltpu.SemaphoreType.DMA((parts, groups)),
            pltpu.SemaphoreType.DMA((2,)),
            pltpu.VMEM((2,) + block, bf16),
            pltpu.SemaphoreType.DMA((2,)),
        ],
        compiler_params=pltpu.CompilerParams(
            collective_id=0, has_side_effects=True, vmem_limit_bytes=36 * 2**20
        ),
        name="channelise_exchange",
    )(samples, coefficients, jnp.asarray(dft_table(length)), jnp.asarray(reorder_matrix()))
    late = per_device - early
    return pl.pallas_call(
        functools.partial(finish_kernel, tm_count, input_count),
        out_shape=jax.ShapeDtypeStruct((per_device, 2, width, width), bf16),
        in_specs=[hbm, anywhere],
        out_specs=hbm,
        scratch_shapes=[
            pltpu.VMEM((late,) + block, bf16),
            pltpu.VMEM((late, 2, width, width), bf16),
            pltpu.SemaphoreType.DMA((late,)),
            pltpu.SemaphoreType.DMA((per_device,)),
        ],
        compiler_params=pltpu.CompilerParams(vmem_limit_bytes=33 * 2**20),
        name="correlate_rest",
    )(received, pltpu.with_memory_space_constraint(products, pltpu.VMEM))


def solution(mesh):
    in_specs = (P("input", "tm"), P())
    out_specs = P(("tm", "input"), None, None, None)
    return jax.shard_map(local, mesh=mesh, in_specs=in_specs, out_specs=out_specs, check_vma=False)
```
